32 devices in a mesh: member: 2 (over y), tile: 4 (over z), tm: 2 (over x), level: 2 (over core).
Axes of the slice: x: 2, y: 2, z: 4, core: 2. Of those that a mesh axis runs over, the one named last changes fastest.
Arguments:
- control: float32 [32, 64, 1536], P(('member', 'level'), ('tile', 'tm')), parts along dimension 0, may hold values from -6 to 6
- residual: float32 [32, 64, 1536], P(('member', 'level'), ('tile', 'tm')), parts along dimension 0, may hold values from -6 to 6
- direction: float32 [32, 64, 1536], P(('member', 'level'), ('tile', 'tm')), parts along dimension 0, may hold values from -6 to 6
- sigma: float32 [32, 64, 1536], P(('member', 'level'), ('tile', 'tm')), parts along dimension 0, may hold values from 0.3 to 3
- decay_rate: float32 [32], P(('member', 'level')), parts along dimension 0, may hold values from 0.005 to 0.4
- obs_cell: int32 [32, 8, 128], P(('member', 'tile'), 'tm'), parts along dimension 0, may hold values from 0 to 23039
- observation_slot: int32 [32, 8, 128], P(('member', 'tile'), 'tm'), parts along dimension 0, may hold values from 0 to 23
- block_count: int32 [32, 8], P(('member', 'tile'), 'tm'), parts along dimension 0, may hold values from 1 to 128, as said below
- horiz_weight: float32 [32, 8, 4, 128], P(('member', 'tile'), 'tm'), parts along dimension 0, may hold values from 0.05 to 0.45
- vert_weight: float32 [32, 8, 16, 128], P(('member', 'tile'), 'tm', 'level'), parts along dimension 0, may hold values from -2.4 to 2.4
- obs_precision: float32 [32, 8, 128], P(('member', 'tile'), 'tm'), parts along dimension 0, may hold values from 2 to 8
Outputs:
- control_new: float32 [32, 64, 1536], P(('member', 'level'), ('tile', 'tm')), parts along dimension 0
- residual_new: float32 [32, 64, 1536], P(('member', 'level'), ('tile', 'tm')), parts along dimension 0
- updated_direction: float32 [32, 64, 1536], P(('member', 'level'), ('tile', 'tm')), parts along dimension 0
The draws below stay inside these ranges and needn't reach their ends.
There are 2 independent parts, one for each index of `member`. The reference program is written for one: setup_inputs(seed, part) draws one part's arguments, and reference() takes and returns one part's arrays. A program takes and returns all parts, laid end to end along the dimension named above; each array names one. Nothing has to cross between parts.
Inputs may be any that keep to these rules, and one draw needn't show every extreme that they name: `block_count`: every first block of each (a) row, b = 0, is full with 128 rows.
All inputs are finite; a program needn't handle non-finite values.
Results may differ from the reference program's by a relative error of at most 0.000024.
Values sent between devices are 32-bit elements; how exact they have to be, the bound alone decides.
A program may use at most 128 MiB of HBM per device.

```python
import math
import jax
import jax.numpy as jnp

NX = 1536
BLOCKS_PER_TILE = 4
WINDOW_SLOTS = 24
K_DIFF = 4
SPATIAL_TILES = 4
TROWS = 16
NY = 64
LEVELS = 16
N_TM = 2


def draw_block_count(key, part):
    key = jax.random.fold_in(key, 7)
    first, second = jax.random.split(key)
    counts = jax.random.randint(first, (SPATIAL_TILES * SPATIAL_TILES, BLOCKS_PER_TILE * N_TM), 1, 129)
    limits = jax.random.randint(second, (SPATIAL_TILES,), 24, 129)
    counts = jnp.minimum(counts, jnp.tile(limits, SPATIAL_TILES)[:, None])
    return counts.at[:, 0].set(128).astype(jnp.int32)


def draw_vert_weight(key, part):
    key = jax.random.fold_in(key, 11)
    sign_key, size_key = jax.random.split(key)
    shape = (SPATIAL_TILES * SPATIAL_TILES, BLOCKS_PER_TILE * N_TM, LEVELS, 128)
    signs = 2.0 * jax.random.randint(sign_key, (shape[0], shape[1], 1, 128), 0, 2).astype(jnp.float32) - 1.0
    magnitude = 1.5 + 0.45 * jnp.clip(jax.random.normal(size_key, shape, jnp.float32), -2.0, 2.0)
    return (signs * magnitude).astype(jnp.float32)


def set_ends(result, own_key, least, largest):
    longest = result.shape.index(max(result.shape))
    spots = []
    for shift in (0, 1):
        where = [jax.random.randint(jax.random.fold_in(own_key, axis), (), 0, length) for axis, length in enumerate(result.shape)]
        where[longest] = (where[longest] + shift) % result.shape[longest]
        spots.append(tuple(where))
    return result.at[spots[0]].set(least).at[spots[1]].set(largest)


def block_levels(rng, dims, pieces, low, largest):
    def one(position, blocks):
        heights = jax.random.uniform(jax.random.fold_in(jax.random.fold_in(rng, 6), position), (blocks,), jnp.float32, low / len(pieces), largest / len(pieces))
        return jnp.repeat(jnp.exp(heights), dims[position] // blocks).reshape((-1,) + (1,) * (len(dims) - position - 1))

    level = one(*pieces[0])
    for cut in pieces[1:]:
        level = level * one(*cut)
    return level


def gaussian(own_key, dims, spread, reach, cuts=(), held_as=jnp.bfloat16):
    loudness = block_levels(own_key, dims, cuts, -0.22, 0.18) if cuts else 1.0
    entries = jax.random.normal(own_key, dims, jnp.float32) * spread * loudness
    return jnp.minimum(jnp.maximum(entries, -reach), reach).astype(held_as)


def setup_inputs(seed: int = 0, part: int = 0) -> dict:
    seeds = jax.random.split(jax.random.key(seed), 12)
    part_splits = jax.random.split(jax.random.fold_in(seeds[11], part), 12)
    return {
        "control": gaussian(part_splits[0], (LEVELS, NY, NX), 1.0, 6.0, ((0, 2), (1, 8)), jnp.float32),
        "residual": gaussian(part_splits[1], (LEVELS, NY, NX), 1.0, 6.0, ((0, 2), (1, 8)), jnp.float32),
        "direction": gaussian(part_splits[2], (LEVELS, NY, NX), 1.0, 6.0, ((0, 2), (1, 8)), jnp.float32),
        "sigma": jnp.clip(jnp.exp(math.log(3.0) - 2.3025851 * jax.random.uniform(part_splits[3], (LEVELS, NY, NX), jnp.float32) ** block_levels(part_splits[3], (LEVELS, NY, NX), ((0, 2), (1, 8)), -0.2, 0.2)), 0.3, 3.0),
        "decay_rate": jnp.clip(jnp.exp(math.log(0.4) - 4.3820267 * jax.random.uniform(part_splits[4], (LEVELS,), jnp.float32) ** block_levels(part_splits[4], (LEVELS,), ((0, 2),), -0.2, 0.2)), 0.005, 0.4),
        "obs_cell": set_ends(jax.random.randint(part_splits[5], (SPATIAL_TILES * SPATIAL_TILES, BLOCKS_PER_TILE * N_TM, 128), 0, (TROWS - 1) * NX), jax.random.fold_in(part_splits[5], 1), 0, ((TROWS - 1) * NX) - 1).astype(jnp.int32),
        "observation_slot": set_ends(jax.random.randint(part_splits[6], (SPATIAL_TILES * SPATIAL_TILES, BLOCKS_PER_TILE * N_TM, 128), 0, WINDOW_SLOTS), jax.random.fold_in(part_splits[6], 1), 0, WINDOW_SLOTS - 1).astype(jnp.int32),
        "block_count": draw_block_count(jax.random.fold_in(jax.random.fold_in(seeds[11], part), 71), part),
        "horiz_weight": jnp.clip(0.05 + 0.39999999 * jax.random.uniform(part_splits[8], (SPATIAL_TILES * SPATIAL_TILES, BLOCKS_PER_TILE * N_TM, 4, 128), jnp.float32) ** block_levels(part_splits[8], (SPATIAL_TILES * SPATIAL_TILES, BLOCKS_PER_TILE * N_TM, 4, 128), ((0, 4), (1, 2)), -0.2, 0.2), 0.05, 0.45),
        "vert_weight": draw_vert_weight(jax.random.fold_in(jax.random.fold_in(seeds[11], part), 71), part),
        "obs_precision": jnp.clip(jnp.exp(math.log(8.0) - 1.3862944 * jax.random.uniform(part_splits[10], (SPATIAL_TILES * SPATIAL_TILES, BLOCKS_PER_TILE * N_TM, 128), jnp.float32) ** block_levels(part_splits[10], (SPATIAL_TILES * SPATIAL_TILES, BLOCKS_PER_TILE * N_TM, 128), ((0, 4), (1, 2)), -0.2, 0.2)), 2.0, 8.0),
    }


center_coef = 0.1
row_coef = 0.2
level_coef = 0.05


def smooth(field):
    for step in range(K_DIFF):
        padded = jnp.pad(field, ((1, 1), (1, 1), (0, 0)))
        rows_sum = padded[1:-1, :-2] + padded[1:-1, 2:] + jnp.roll(field, 1, 2) + jnp.roll(field, -1, 2)
        levels_sum = padded[:-2, 1:-1] + padded[2:, 1:-1]
        field = center_coef * field + row_coef * rows_sum + level_coef * levels_sum
    return field


def corners(cell, base, width):
    row = cell // width
    col = cell % width
    right = (col + 1) % width
    first = (base + row) * width
    return (first + col, first + right, first + width + col, first + width + right)


def reference(control, residual, direction, sigma, decay_rate, obs_cell, observation_slot, block_count, horiz_weight, vert_weight, obs_precision):
    increment = sigma * smooth(direction)
    flat = increment.reshape(LEVELS, -1)
    pairs = obs_cell.shape[0]
    dest = (jnp.arange(pairs, dtype=jnp.int32) % SPATIAL_TILES)[:, None, None]
    cells = corners(obs_cell, dest * TROWS, NX)
    eff_weight = vert_weight * jnp.exp(-observation_slot[:, :, None, :].astype(jnp.float32) * decay_rate[None, None, :, None])
    inner = jnp.zeros((LEVELS,) + obs_cell.shape, jnp.float32)
    for k in range(4):
        inner = inner + horiz_weight[:, :, k, :][None] * flat[:, cells[k]]
    model_obs = jnp.sum(eff_weight * jnp.moveaxis(inner, 0, 2), axis=2)
    valid = jnp.arange(128, dtype=jnp.int32)[None, None, :] < block_count[:, :, None]
    innovation_misfit = jnp.where(valid, obs_precision * model_obs, 0.0)
    scaled = jnp.moveaxis(eff_weight * innovation_misfit[:, :, None, :], 2, 0)
    adjoint = jnp.zeros_like(flat)
    for k in range(4):
        values = (scaled * horiz_weight[:, :, k, :][None]).reshape(LEVELS, -1)
        adjoint = adjoint.at[:, cells[k].reshape(-1)].add(values)
    image = direction + smooth(sigma * adjoint.reshape(increment.shape))
    norm_old = jnp.sum(residual * residual)
    alpha = norm_old / jnp.sum(direction * image)
    control_new = control + alpha * direction
    residual_new = residual - alpha * image
    norm_new = jnp.sum(residual_new * residual_new)
    updated_direction = residual_new + (norm_new / norm_old) * direction
    return control_new, residual_new, updated_direction
```

```python
import functools

import jax
import jax.numpy as jnp
from jax import lax
from jax.experimental import pallas as pl
from jax.experimental.pallas import tpu as pltpu
from jax.sharding import PartitionSpec as P

K_DIFF = 4
HALO = K_DIFF
center_coef = 0.1
row_coef = 0.2
level_coef = 0.05
MESH = pl.DeviceIdType.MESH
f32 = jnp.float32
bf16 = jnp.bfloat16


def split(x):
    high = x.astype(bf16)
    return high, (x - high.astype(f32)).astype(bf16)


def kernel(
    sizes,
    residual, direction, sigma, decay, cell, slot, count, horiz, vert, prec,
    image, scal,
    a0, a1, t0, t1, top, bot, rd, ru, xd, xu, xc, pack, obs, fields, parts, models,
    acc, ip1, ip2,
    halo_send, halo_recv, obs_send, obs_recv, mod_send, mod_recv,
    s1_send, s1_recv, s2_send, s2_recv,
):
    nt, ntm, nlev = sizes
    levels, rows, width = direction.shape
    blocks = cell.shape[1]
    ng, ngroup = nt * ntm, ntm * nlev
    member = lax.axis_index("member")
    tile = lax.axis_index("tile")
    tm = lax.axis_index("tm")
    lev = lax.axis_index("level")
    g = tile * ntm + tm
    other = 1 - lev
    has_up, has_down = g > 0, g < ng - 1

    def dev(index, level):
        return (member, index // ntm, lax.rem(index, ntm), level)

    barrier = pltpu.get_barrier_semaphore()
    everyone = ng * nlev
    me = g * nlev + lev
    for i in range(1, everyone):
        to = lax.rem(me + i, everyone)
        pl.semaphore_signal(
            barrier, inc=1, device_id=dev(to // nlev, lax.rem(to, nlev)), device_id_type=MESH
        )

    sub = lax.broadcasted_iota(jnp.int32, (rows, width), 0)
    low_half = sub < HALO

    def pack_rows(source, base):
        for j in range(levels // 2):
            even, odd = source[base + 2 * j], pltpu.roll(source[base + 2 * j + 1], HALO, 0)
            top[j] = jnp.where(low_half, even, odd)
            bot[j] = jnp.where(low_half, odd, even)

    def halo_copies(phase, source, base):
        up, down = g - 1, g + 1
        half = pl.ds(2 * other, 2)
        edge = pl.ds(base + HALO * other, HALO)
        plan = [
            (top, rd.at[phase], up, lev, has_up, has_down),
            (bot, ru.at[phase], down, lev, has_down, has_up),
            (top.at[half], xd.at[phase], up, other, has_up, has_down),
            (bot.at[half], xu.at[phase], down, other, has_down, has_up),
            (source.at[edge], xc.at[phase], g, other, None, None),
        ]
        return [
            (
                pltpu.make_async_remote_copy(
                    src_ref=src, dst_ref=dst,
                    send_sem=halo_send.at[phase, n], recv_sem=halo_recv.at[phase, n],
                    device_id=dev(jnp.clip(to, 0, ng - 1), level), device_id_type=MESH,
                ),
                sends, gets,
            )
            for n, (src, dst, to, level, sends, gets) in enumerate(plan)
        ]

    def when(condition, action):
        if condition is None:
            action()
        else:
            pl.when(condition)(action)

    pack_rows(direction, 0)
    pl.semaphore_wait(barrier, everyone - 1)
    halo1 = halo_copies(0, direction, 0)
    for copy, sends, gets in halo1:
        when(sends, copy.start)

    eff_rows = blocks * levels
    h_rows = eff_rows + blocks * 4
    level_id = lax.broadcasted_iota(jnp.int32, (levels, 128), 0)
    lane = lax.broadcasted_iota(jnp.int32, (1, 128), 1)
    rate = jnp.zeros((levels, 128), f32)
    for l in range(levels):
        rate = jnp.where(level_id == l, decay[l], rate)

    def pack_tile(t, carry):
        for b in range(blocks):
            s = slot[t, b : b + 1, :].astype(f32)
            pack[t, b * levels : (b + 1) * levels, :] = vert[t, b] * jnp.exp(-s * rate)
            pack[t, eff_rows + 4 * b : eff_rows + 4 * b + 4, :] = horiz[t, b]
            pack[t, h_rows + b : h_rows + b + 1, :] = jnp.where(
                lane < count[t, b], prec[t, b : b + 1, :], 0.0
            )
        pack[t, h_rows + blocks : h_rows + 2 * blocks, :] = cell[t].astype(f32)
        return carry

    lax.fori_loop(0, nt, pack_tile, 0)

    def obs_copy(i):
        to = lax.rem(g + i, ng)
        return pltpu.make_async_remote_copy(
            src_ref=pack.at[to // ntm], dst_ref=obs.at[g],
            send_sem=obs_send.at[i], recv_sem=obs_recv.at[i],
            device_id=dev(to, lev), device_id_type=MESH,
        )

    def obs_arrival(i):
        return pltpu.make_async_remote_copy(
            src_ref=pack.at[tile], dst_ref=obs.at[lax.rem(g - i + ng, ng)],
            send_sem=obs_send.at[i], recv_sem=obs_recv.at[i],
            device_id=dev(lax.rem(g + i, ng), lev), device_id_type=MESH,
        )

    for i in range(1, ng):
        obs_copy(i).start()
    obs[g] = pack[tile]

    inside = (low_half & has_down) | (jnp.logical_not(low_half) & has_up)

    def unpack(down, up, n, base):
        for j in range(n):
            a1[base + 2 * j] = jnp.where(inside, jnp.where(low_half, down[j], up[j]), 0.0)
            a1[base + 2 * j + 1] = jnp.where(
                inside, pltpu.roll(jnp.where(low_half, up[j], down[j]), HALO, 0), 0.0
            )

    zero = jnp.zeros((rows, width), f32)
    for buffer in (a0, a1, t0, t1):
        buffer[0] = zero
        buffer[levels + HALO + 1] = zero
    own = 1 + HALO * lev
    far = 1 + levels * other

    def receive(phase, copies):
        for copy, sends, gets in copies:
            when(gets, copy.wait_recv)
        unpack(rd.at[phase], ru.at[phase], levels // 2, own)
        unpack(xd.at[phase], xu.at[phase], HALO // 2, far)
        for l in range(HALO):
            a0[far + l] = xc[phase, l]
        for copy, sends, gets in copies:
            when(sends, copy.wait_send)

    def smooth_step(step, src0, src1, dst0, dst1):
        def body(i, carry):
            l = 1 + step * lev + i
            full = jnp.concatenate([src0[l], src1[l]], axis=0)
            near = (
                pltpu.roll(full, 1, 0) + pltpu.roll(full, 2 * rows - 1, 0)
                + pltpu.roll(full, 1, 1) + pltpu.roll(full, width - 1, 1)
            )
            main = center_coef * full + row_coef * near
            dst0[l] = main[:rows] + level_coef * (src0[l - 1] + src0[l + 1])
            if step < K_DIFF:
                side = main[rows:] + level_coef * (src1[l - 1] + src1[l + 1])
                dst1[l] = jnp.where(inside, side, 0.0)
            return carry

        lax.fori_loop(0, levels + HALO - step, body, 0)

    def smooth():
        smooth_step(1, a0, a1, t0, t1)
        smooth_step(2, t0, t1, a0, a1)
        smooth_step(3, a0, a1, t0, t1)
        smooth_step(4, t0, t1, a0, a1)

    a0[pl.ds(own, levels)] = direction[...]
    receive(0, halo1)
    smooth()

    cells_here = levels * rows
    increment = (sigma[...] * a0[pl.ds(own, levels)]).reshape(cells_here, width)
    high, low = split(increment)
    fields[0:cells_here] = high
    fields[2 * cells_here : 3 * cells_here] = low
    high, low = split(pltpu.roll(increment, width - 1, 1))
    fields[cells_here : 2 * cells_here] = high
    fields[3 * cells_here : 4 * cells_here] = low

    for i in range(1, ng):
        obs_arrival(i).wait_recv()

    nobs = blocks * 128
    row_id = lax.broadcasted_iota(jnp.int32, (rows, nobs), 0).astype(f32)
    first_row = (tm * rows).astype(f32)

    def lanes(q, start, stride):
        return jnp.concatenate(
            [obs[q, start + b * stride : start + b * stride + 1, :] for b in range(blocks)], axis=1
        )

    def stencil(q):
        c = lanes(q, h_rows + blocks, 1)
        row = jnp.floor((c + 0.5) * (1.0 / width))
        col = (c - row * width).astype(jnp.int32)
        row = row - first_row
        lower, upper = row_id == row, row_id == row + 1.0
        weights = [
            jnp.where(lower, lanes(q, eff_rows + k, 4), 0.0)
            + jnp.where(upper, lanes(q, eff_rows + 2 + k, 4), 0.0)
            for k in range(2)
        ]
        col_id = lax.broadcasted_iota(jnp.int32, (width, nobs), 0)
        onehot = jnp.where(col_id == col, 1.0, 0.0).astype(bf16)
        return weights, onehot

    def gather(q, carry):
        weights, onehot = stencil(q)
        values = jnp.dot(fields[...], onehot, preferred_element_type=f32)
        values = values[: 2 * cells_here] + values[2 * cells_here :]
        total = jnp.zeros((rows, nobs), f32)
        for k in range(2):
            part = jnp.zeros((rows, nobs), f32)
            for l in range(levels):
                at = k * cells_here + l * rows
                part = part + lanes(q, l, levels) * values[at : at + rows]
            total = total + part * weights[k]
        total = jnp.sum(total, axis=0, keepdims=True)
        parts[q] = jnp.concatenate(
            [total[:, 128 * b : 128 * (b + 1)] for b in range(blocks)]
            + [jnp.zeros((8 - blocks, 128), f32)],
            axis=0,
        )
        return carry

    lax.fori_loop(0, ng, gather, 0)

    tg = tm * nlev + lev

    def exchange(i, src, slots, send, recv):
        to = lax.rem(tg + i, ngroup)
        came = lax.rem(tg - i + ngroup, ngroup)
        where = (member, tile, to // nlev, lax.rem(to, nlev))
        return [
            pltpu.make_async_remote_copy(
                src_ref=src, dst_ref=slots.at[at], send_sem=send.at[i], recv_sem=recv.at[i],
                device_id=where, device_id_type=MESH,
            )
            for at in (tg, came)
        ]

    swaps = [exchange(i, parts, models, mod_send, mod_recv) for i in range(1, ngroup)]
    for out, _ in swaps:
        out.start()
    models[tg] = parts[...]
    acc[...] = jnp.zeros_like(acc)
    for _, back in swaps:
        back.wait_recv()

    def scatter(q, carry):
        weights, onehot = stencil(q)
        model = models[0, q]
        for k in range(1, ngroup):
            model = model + models[k, q]
        departure = jnp.concatenate([model[b : b + 1] for b in range(blocks)], axis=1)
        departure = departure * lanes(q, h_rows, 1)
        scaled = [lanes(q, l, levels) * departure for l in range(levels)]
        values = jnp.concatenate(
            [scaled[l] * weights[k] for k in range(2) for l in range(levels)], axis=0
        )
        acc[...] += lax.dot_general(
            jnp.concatenate(split(values), axis=0), onehot, (((1,), (1,)), ((), ())),
            preferred_element_type=f32,
        )
        return carry

    lax.fori_loop(0, ng, scatter, 0)
    adjoint = acc[: 2 * cells_here] + acc[2 * cells_here :]
    adjoint = adjoint[:cells_here] + pltpu.roll(adjoint[cells_here:], 1, 1)
    a0[pl.ds(own, levels)] = sigma[...] * adjoint.reshape(levels, rows, width)
    pack_rows(a0, own)
    halo2 = halo_copies(1, a0, own)
    for copy, sends, gets in halo2:
        when(sends, copy.start)
    receive(1, halo2)
    smooth()

    sums = [jnp.zeros((rows, width), f32)] * 4
    for l in range(levels):
        d, r = direction[l], residual[l]
        im = d + a0[own + l]
        image[l] = im
        for n, term in enumerate((r * r, d * im, r * im, im * im)):
            sums[n] = sums[n] + term
    lines = []
    for total in sums:
        total = jnp.sum(total, axis=0, keepdims=True)
        line = total[:, :128]
        for at in range(128, width, 128):
            line = line + total[:, at : at + 128]
        lines.append(line)
    ip1[tg] = jnp.concatenate(lines + [jnp.zeros((4, 128), f32)], axis=0)
    swaps1 = [exchange(i, ip1.at[tg], ip1, s1_send, s1_recv) for i in range(1, ngroup)]
    for out, _ in swaps1:
        out.start()
    for _, back in swaps1:
        back.wait_recv()
    total = ip1[0]
    for k in range(1, ngroup):
        total = total + ip1[k]
    ip2[tile] = total
    swaps2 = []
    for i in range(1, nt):
        swaps2.append(
            [
                pltpu.make_async_remote_copy(
                    src_ref=ip2.at[tile], dst_ref=ip2.at[at],
                    send_sem=s2_send.at[i], recv_sem=s2_recv.at[i],
                    device_id=(member, lax.rem(tile + i, nt), tm, lev), device_id_type=MESH,
                )
                for at in (tile, lax.rem(tile - i + nt, nt))
            ]
        )
    for out, _ in swaps2:
        out.start()
    for _, back in swaps2:
        back.wait_recv()
    total = ip2[0]
    for k in range(1, nt):
        total = total + ip2[k]
    total = jnp.broadcast_to(jnp.sum(total, axis=1, keepdims=True), (8, 128))
    norm_old, curvature, cross, image_norm = (total[n : n + 1] for n in range(4))
    alpha = norm_old / curvature
    norm_new = norm_old - 2.0 * alpha * cross + alpha * alpha * image_norm
    scal[...] = jnp.concatenate([alpha, norm_new / norm_old, jnp.zeros((6, 128), f32)], axis=0)

    for i in range(1, ng):
        obs_copy(i).wait_send()
    for out, _ in swaps + swaps1 + swaps2:
        out.wait_send()


def local(
    sizes,
    control,
    residual,
    direction,
    sigma,
    decay_rate,
    obs_cell,
    observation_slot,
    block_count,
    horiz_weight,
    vert_weight,
    obs_precision,
):
    nt, ntm, nlev = sizes
    levels, rows, width = direction.shape
    blocks = obs_cell.shape[1]
    ng, ngroup = nt * ntm, ntm * nlev
    packed = blocks * (levels + 6)
    vmem = pl.BlockSpec(memory_space=pltpu.VMEM)
    smem = pl.BlockSpec(memory_space=pltpu.SMEM)
    field = pltpu.VMEM((levels + HALO + 2, rows, width), f32)
    dma = pltpu.SemaphoreType.DMA
    image, scal = pl.pallas_call(
        functools.partial(kernel, sizes),
        out_shape=(
            jax.ShapeDtypeStruct((levels, rows, width), f32),
            jax.ShapeDtypeStruct((8, 128), f32),
        ),
        in_specs=[vmem, vmem, vmem, smem, vmem, vmem, smem, vmem, vmem, vmem],
        out_specs=(vmem, vmem),
        scratch_shapes=[
            field, field, field, field,
            pltpu.VMEM((levels // 2, rows, width), f32),
            pltpu.VMEM((levels // 2, rows, width), f32),
            pltpu.VMEM((2, levels // 2, rows, width), f32),
            pltpu.VMEM((2, levels // 2, rows, width), f32),
            pltpu.VMEM((2, HALO // 2, rows, width), f32),
            pltpu.VMEM((2, HALO // 2, rows, width), f32),
            pltpu.VMEM((2, HALO, rows, width), f32),
            pltpu.VMEM((nt, packed, 128), f32),
            pltpu.VMEM((ng, packed, 128), f32),
            pltpu.VMEM((4 * levels * rows, width), bf16),
            pltpu.VMEM((ng, 8, 128), f32),
            pltpu.VMEM((ngroup, ng, 8, 128), f32),
            pltpu.VMEM((4 * levels * rows, width), f32),
            pltpu.VMEM((ngroup, 8, 128), f32),
            pltpu.VMEM((nt, 8, 128), f32),
            dma((2, 5)), dma((2, 5)),
            dma((ng,)), dma((ng,)),
            dma((ngroup,)), dma((ngroup,)),
            dma((ngroup,)), dma((ngroup,)),
            dma((nt,)), dma((nt,)),
        ],
        compiler_params=pltpu.CompilerParams(
            collective_id=0, has_side_effects=True, vmem_limit_bytes=48 * 1024 * 1024
        ),
    )(
        residual, direction, sigma, decay_rate, obs_cell, observation_slot, block_count,
        horiz_weight, vert_weight, obs_precision,
    )
    alpha, beta = scal[0, 0], scal[1, 0]
    residual_new = residual - alpha * image
    control_new = control + alpha * direction
    updated_direction = residual_new + beta * direction
    return (control_new, residual_new, updated_direction)


def solution(mesh):
    grid = P(("member", "level"), ("tile", "tm"), None)
    placed = (
        grid,
        grid,
        grid,
        grid,
        P(("member", "level")),
        P(("member", "tile"), "tm", None),
        P(("member", "tile"), "tm", None),
        P(("member", "tile"), "tm"),
        P(("member", "tile"), "tm", None, None),
        P(("member", "tile"), "tm", "level", None),
        P(("member", "tile"), "tm", None),
    )
    sizes = tuple(mesh.shape[axis] for axis in ("tile", "tm", "level"))
    return jax.shard_map(
        functools.partial(local, sizes),
        mesh=mesh,
        in_specs=placed,
        out_specs=(grid, grid, grid),
        check_vma=False,
    )
```

```python
import functools

import jax
import jax.numpy as jnp
from jax import lax
from jax.experimental import pallas as pl
from jax.experimental.pallas import tpu as pltpu
from jax.sharding import PartitionSpec as P

K_DIFF = 4
HALO = K_DIFF
center_coef = 0.1
row_coef = 0.2
level_coef = 0.05
MESH = pl.DeviceIdType.MESH
f32 = jnp.float32
bf16 = jnp.bfloat16


def split(x):
    high = x.astype(bf16)
    return high, (x - high.astype(f32)).astype(bf16)


def kernel(
    sizes,
    residual_h, direction_h, sigma_h, decay, cell_h, slot_h, count, horiz_h, vert_h, prec_h,
    image, scal,
    residual, direction, sigma, cell, slot, horiz, vert, prec, onehots, load_sem,
    a0, a1, t0, t1, top, bot, rd, ru, xd, xu, xc, pack, obs, fields, parts, models,
    acc, ip1, ip2,
    halo_send, halo_recv, obs_send, obs_recv, mod_send, mod_recv,
    s1_send, s1_recv, s2_send, s2_recv,
):
    nt, ntm, nlev = sizes
    levels, rows, width = direction.shape
    blocks = cell.shape[1]
    ng, ngroup = nt * ntm, ntm * nlev
    keep = onehots.shape[0] > 1
    member = lax.axis_index("member")
    tile = lax.axis_index("tile")
    tm = lax.axis_index("tm")
    lev = lax.axis_index("level")
    g = tile * ntm + tm
    other = 1 - lev
    has_up, has_down = g > 0, g < ng - 1

    def dev(index, level):
        return (member, index // ntm, lax.rem(index, ntm), level)

    loads = [
        pltpu.make_async_copy(src, dst, load_sem.at[n])
        for n, (src, dst) in enumerate(
            [
                (direction_h, direction), (vert_h, vert), (horiz_h, horiz), (cell_h, cell),
                (slot_h, slot), (prec_h, prec), (sigma_h, sigma), (residual_h, residual),
            ]
        )
    ]
    for load in loads:
        load.start()

    barrier = pltpu.get_barrier_semaphore()
    everyone = ng * nlev
    me = g * nlev + lev
    for i in range(1, everyone):
        to = lax.rem(me + i, everyone)
        pl.semaphore_signal(
            barrier, inc=1, device_id=dev(to // nlev, lax.rem(to, nlev)), device_id_type=MESH
        )

    sub = lax.broadcasted_iota(jnp.int32, (rows, width), 0)
    low_half = sub < HALO

    def pack_rows(source, base):
        for j in range(levels // 2):
            even, odd = source[base + 2 * j], pltpu.roll(source[base + 2 * j + 1], HALO, 0)
            top[j] = jnp.where(low_half, even, odd)
            bot[j] = jnp.where(low_half, odd, even)

    def halo_copies(phase, source, base):
        up, down = g - 1, g + 1
        half = pl.ds(2 * other, 2)
        edge = pl.ds(base + HALO * other, HALO)
        plan = [
            (top, rd.at[phase], up, lev, has_up, has_down),
            (bot, ru.at[phase], down, lev, has_down, has_up),
            (source.at[edge], xc.at[phase], g, other, None, None),
            (rd.at[phase].at[half], xd.at[phase], g, other, has_down, has_down),
            (ru.at[phase].at[half], xu.at[phase], g, other, has_up, has_up),
        ]
        return [
            (
                pltpu.make_async_remote_copy(
                    src_ref=src, dst_ref=dst,
                    send_sem=halo_send.at[phase, n], recv_sem=halo_recv.at[phase, n],
                    device_id=dev(jnp.clip(to, 0, ng - 1), level), device_id_type=MESH,
                ),
                sends, gets,
            )
            for n, (src, dst, to, level, sends, gets) in enumerate(plan)
        ]

    def when(condition, action):
        if condition is None:
            action()
        else:
            pl.when(condition)(action)

    loads[0].wait()
    pack_rows(direction, 0)
    for load in loads[1:6]:
        load.wait()

    eff_rows = blocks * levels
    h_rows = eff_rows + blocks * 4
    level_id = lax.broadcasted_iota(jnp.int32, (levels, 128), 0)
    lane = lax.broadcasted_iota(jnp.int32, (1, 128), 1)
    rate = jnp.zeros((levels, 128), f32)
    for l in range(levels):
        rate = jnp.where(level_id == l, decay[l], rate)

    def pack_tile(t, carry):
        for b in range(blocks):
            s = slot[t, b : b + 1, :].astype(f32)
            pack[t, b * levels : (b + 1) * levels, :] = vert[t, b] * jnp.exp(-s * rate)
            pack[t, eff_rows + 4 * b : eff_rows + 4 * b + 4, :] = horiz[t, b]
            pack[t, h_rows + b : h_rows + b + 1, :] = jnp.where(
                lane < count[t, b], prec[t, b : b + 1, :], 0.0
            )
        pack[t, h_rows + blocks : h_rows + 2 * blocks, :] = cell[t].astype(f32)
        return carry

    lax.fori_loop(0, nt, pack_tile, 0)
    pl.semaphore_wait(barrier, everyone - 1)
    halo1 = halo_copies(0, direction, 0)
    for copy, sends, gets in halo1[:3]:
        when(sends, copy.start)

    def obs_copy(i):
        to = lax.rem(g + i, ng)
        return pltpu.make_async_remote_copy(
            src_ref=pack.at[to // ntm], dst_ref=obs.at[g],
            send_sem=obs_send.at[i], recv_sem=obs_recv.at[i],
            device_id=dev(to, lev), device_id_type=MESH,
        )

    def obs_arrival(i):
        return pltpu.make_async_remote_copy(
            src_ref=pack.at[tile], dst_ref=obs.at[lax.rem(g - i + ng, ng)],
            send_sem=obs_send.at[i], recv_sem=obs_recv.at[i],
            device_id=dev(lax.rem(g + i, ng), lev), device_id_type=MESH,
        )

    for i in range(1, ng):
        obs_copy(i).start()
    obs[g] = pack[tile]

    inside = (low_half & has_down) | (jnp.logical_not(low_half) & has_up)

    def unpack(down, up, n, base):
        for j in range(n):
            a1[base + 2 * j] = jnp.where(inside, jnp.where(low_half, down[j], up[j]), 0.0)
            a1[base + 2 * j + 1] = jnp.where(
                inside, pltpu.roll(jnp.where(low_half, up[j], down[j]), HALO, 0), 0.0
            )

    zero = jnp.zeros((rows, width), f32)
    for buffer in (a0, a1, t0, t1):
        buffer[0] = zero
        buffer[levels + HALO + 1] = zero
    own = 1 + HALO * lev
    far = 1 + levels * other

    def receive(phase, copies):
        for n in range(2):
            when(copies[n][2], copies[n][0].wait_recv)
            when(copies[3 + n][1], copies[3 + n][0].start)
        unpack(rd.at[phase], ru.at[phase], levels // 2, own)
        for copy, sends, gets in copies[2:]:
            when(gets, copy.wait_recv)
        unpack(xd.at[phase], xu.at[phase], HALO // 2, far)
        for l in range(HALO):
            a0[far + l] = xc[phase, l]
        for copy, sends, gets in copies:
            when(sends, copy.wait_send)

    def smooth_step(step, src0, src1, dst0, dst1):
        def body(i, carry):
            l = 1 + step * lev + i
            full = jnp.concatenate([src0[l], src1[l]], axis=0)
            near = (
                pltpu.roll(full, 1, 0) + pltpu.roll(full, 2 * rows - 1, 0)
                + pltpu.roll(full, 1, 1) + pltpu.roll(full, width - 1, 1)
            )
            main = center_coef * full + row_coef * near
            dst0[l] = main[:rows] + level_coef * (src0[l - 1] + src0[l + 1])
            if step < K_DIFF:
                side = main[rows:] + level_coef * (src1[l - 1] + src1[l + 1])
                dst1[l] = jnp.where(inside, side, 0.0)
            return carry

        lax.fori_loop(0, levels + HALO - step, body, 0)

    def smooth():
        smooth_step(1, a0, a1, t0, t1)
        smooth_step(2, t0, t1, a0, a1)
        smooth_step(3, a0, a1, t0, t1)
        smooth_step(4, t0, t1, a0, a1)

    a0[pl.ds(own, levels)] = direction[...]
    receive(0, halo1)
    smooth()

    loads[6].wait()
    cells_here = levels * rows
    increment = (sigma[...] * a0[pl.ds(own, levels)]).reshape(cells_here, width)
    high, low = split(increment)
    fields[0:cells_here] = high
    fields[2 * cells_here : 3 * cells_here] = low
    high, low = split(pltpu.roll(increment, width - 1, 1))
    fields[cells_here : 2 * cells_here] = high
    fields[3 * cells_here : 4 * cells_here] = low

    for i in range(1, ng):
        obs_arrival(i).wait_recv()

    nobs = blocks * 128
    row_id = lax.broadcasted_iota(jnp.int32, (rows, nobs), 0).astype(f32)
    first_row = (tm * rows).astype(f32)

    def lanes(q, start, stride):
        return jnp.concatenate(
            [obs[q, start + b * stride : start + b * stride + 1, :] for b in range(blocks)], axis=1
        )

    def stencil(q):
        c = lanes(q, h_rows + blocks, 1)
        row = jnp.floor((c + 0.5) * (1.0 / width))
        col = (c - row * width).astype(jnp.int32)
        row = row - first_row
        lower, upper = row_id == row, row_id == row + 1.0
        weights = [
            jnp.where(lower, lanes(q, eff_rows + k, 4), 0.0)
            + jnp.where(upper, lanes(q, eff_rows + 2 + k, 4), 0.0)
            for k in range(2)
        ]
        return weights, col

    def matrix(col):
        col_id = lax.broadcasted_iota(jnp.int32, (width, nobs), 0)
        return jnp.where(col_id == col, 1.0, 0.0).astype(bf16)

    def gather(q, carry):
        weights, col = stencil(q)
        onehot = matrix(col)
        if keep:
            onehots[q] = onehot
        values = jnp.dot(fields[...], onehot, preferred_element_type=f32)
        values = values[: 2 * cells_here] + values[2 * cells_here :]
        total = jnp.zeros((rows, nobs), f32)
        for k in range(2):
            part = jnp.zeros((rows, nobs), f32)
            for l in range(levels):
                at = k * cells_here + l * rows
                part = part + lanes(q, l, levels) * values[at : at + rows]
            total = total + part * weights[k]
        total = jnp.sum(total, axis=0, keepdims=True)
        parts[q] = jnp.concatenate(
            [total[:, 128 * b : 128 * (b + 1)] for b in range(blocks)]
            + [jnp.zeros((8 - blocks, 128), f32)],
            axis=0,
        )
        return carry

    lax.fori_loop(0, ng, gather, 0)

    tg = tm * nlev + lev

    def exchange(i, src, slots, send, recv):
        to = lax.rem(tg + i, ngroup)
        came = lax.rem(tg - i + ngroup, ngroup)
        where = (member, tile, to // nlev, lax.rem(to, nlev))
        return [
            pltpu.make_async_remote_copy(
                src_ref=src, dst_ref=slots.at[at], send_sem=send.at[i], recv_sem=recv.at[i],
                device_id=where, device_id_type=MESH,
            )
            for at in (tg, came)
        ]

    swaps = [exchange(i, parts, models, mod_send, mod_recv) for i in range(1, ngroup)]
    for out, _ in swaps:
        out.start()
    models[tg] = parts[...]
    acc[...] = jnp.zeros_like(acc)
    for _, back in swaps:
        back.wait_recv()

    def scatter(q, carry):
        weights, col = stencil(q)
        onehot = onehots[q] if keep else matrix(col)
        model = models[0, q]
        for k in range(1, ngroup):
            model = model + models[k, q]
        departure = jnp.concatenate([model[b : b + 1] for b in range(blocks)], axis=1)
        departure = departure * lanes(q, h_rows, 1)
        scaled = [lanes(q, l, levels) * departure for l in range(levels)]
        values = jnp.concatenate(
            [scaled[l] * weights[k] for k in range(2) for l in range(levels)], axis=0
        )
        acc[...] += lax.dot_general(
            jnp.concatenate(split(values), axis=0), onehot, (((1,), (1,)), ((), ())),
            preferred_element_type=f32,
        )
        return carry

    lax.fori_loop(0, ng, scatter, 0)
    adjoint = acc[: 2 * cells_here] + acc[2 * cells_here :]
    adjoint = adjoint[:cells_here] + pltpu.roll(adjoint[cells_here:], 1, 1)
    a0[pl.ds(own, levels)] = sigma[...] * adjoint.reshape(levels, rows, width)
    pack_rows(a0, own)
    halo2 = halo_copies(1, a0, own)
    for copy, sends, gets in halo2[:3]:
        when(sends, copy.start)
    receive(1, halo2)
    smooth()

    loads[7].wait()
    sums = [jnp.zeros((rows, width), f32)] * 4
    for l in range(levels):
        d, r = direction[l], residual[l]
        im = d + a0[own + l]
        image[l] = im
        for n, term in enumerate((r * r, d * im, r * im, im * im)):
            sums[n] = sums[n] + term
    lines = []
    for total in sums:
        total = jnp.sum(total, axis=0, keepdims=True)
        line = total[:, :128]
        for at in range(128, width, 128):
            line = line + total[:, at : at + 128]
        lines.append(line)
    ip1[tg] = jnp.concatenate(lines + [jnp.zeros((4, 128), f32)], axis=0)
    swaps1 = [exchange(i, ip1.at[tg], ip1, s1_send, s1_recv) for i in range(1, ngroup)]
    for out, _ in swaps1:
        out.start()
    for _, back in swaps1:
        back.wait_recv()
    total = ip1[0]
    for k in range(1, ngroup):
        total = total + ip1[k]
    ip2[tile] = total
    swaps2 = []
    for i in range(1, nt):
        swaps2.append(
            [
                pltpu.make_async_remote_copy(
                    src_ref=ip2.at[tile], dst_ref=ip2.at[at],
                    send_sem=s2_send.at[i], recv_sem=s2_recv.at[i],
                    device_id=(member, lax.rem(tile + i, nt), tm, lev), device_id_type=MESH,
                )
                for at in (tile, lax.rem(tile - i + nt, nt))
            ]
        )
    for out, _ in swaps2:
        out.start()
    for _, back in swaps2:
        back.wait_recv()
    total = ip2[0]
    for k in range(1, nt):
        total = total + ip2[k]
    total = jnp.broadcast_to(jnp.sum(total, axis=1, keepdims=True), (8, 128))
    norm_old, curvature, cross, image_norm = (total[n : n + 1] for n in range(4))
    alpha = norm_old / curvature
    norm_new = norm_old - 2.0 * alpha * cross + alpha * alpha * image_norm
    scal[...] = jnp.concatenate([alpha, norm_new / norm_old, jnp.zeros((6, 128), f32)], axis=0)

    for i in range(1, ng):
        obs_copy(i).wait_send()
    for out, _ in swaps + swaps1 + swaps2:
        out.wait_send()


def local(
    sizes,
    control,
    residual,
    direction,
    sigma,
    decay_rate,
    obs_cell,
    observation_slot,
    block_count,
    horiz_weight,
    vert_weight,
    obs_precision,
):
    nt, ntm, nlev = sizes
    levels, rows, width = direction.shape
    blocks = obs_cell.shape[1]
    ng, ngroup = nt * ntm, ntm * nlev
    packed = blocks * (levels + 6)
    vmem = pl.BlockSpec(memory_space=pltpu.VMEM)
    hbm = pl.BlockSpec(memory_space=pl.ANY)
    matrices = ng if ng * width * blocks * 128 <= 2**23 else 1
    smem = pl.BlockSpec(memory_space=pltpu.SMEM)
    field = pltpu.VMEM((levels + HALO + 2, rows, width), f32)
    dma = pltpu.SemaphoreType.DMA
    image, scal = pl.pallas_call(
        functools.partial(kernel, sizes),
        out_shape=(
            jax.ShapeDtypeStruct((levels, rows, width), f32),
            jax.ShapeDtypeStruct((8, 128), f32),
        ),
        in_specs=[hbm, hbm, hbm, smem, hbm, hbm, smem, hbm, hbm, hbm],
        out_specs=(vmem, vmem),
        scratch_shapes=[
            *(
                pltpu.VMEM(x.shape, x.dtype)
                for x in (
                    residual, direction, sigma, obs_cell, observation_slot,
                    horiz_weight, vert_weight, obs_precision,
                )
            ),
            pltpu.VMEM((matrices, width, blocks * 128), bf16),
            pltpu.SemaphoreType.DMA((8,)),
            field, field, field, field,
            pltpu.VMEM((levels // 2, rows, width), f32),
            pltpu.VMEM((levels // 2, rows, width), f32),
            pltpu.VMEM((2, levels // 2, rows, width), f32),
            pltpu.VMEM((2, levels // 2, rows, width), f32),
            pltpu.VMEM((2, HALO // 2, rows, width), f32),
            pltpu.VMEM((2, HALO // 2, rows, width), f32),
            pltpu.VMEM((2, HALO, rows, width), f32),
            pltpu.VMEM((nt, packed, 128), f32),
            pltpu.VMEM((ng, packed, 128), f32),
            pltpu.VMEM((4 * levels * rows, width), bf16),
            pltpu.VMEM((ng, 8, 128), f32),
            pltpu.VMEM((ngroup, ng, 8, 128), f32),
            pltpu.VMEM((4 * levels * rows, width), f32),
            pltpu.VMEM((ngroup, 8, 128), f32),
            pltpu.VMEM((nt, 8, 128), f32),
            dma((2, 5)), dma((2, 5)),
            dma((ng,)), dma((ng,)),
            dma((ngroup,)), dma((ngroup,)),
            dma((ngroup,)), dma((ngroup,)),
            dma((nt,)), dma((nt,)),
        ],
        compiler_params=pltpu.CompilerParams(
            collective_id=0, has_side_effects=True, vmem_limit_bytes=60 * 1024 * 1024
        ),
    )(
        residual, direction, sigma, decay_rate, obs_cell, observation_slot, block_count,
        horiz_weight, vert_weight, obs_precision,
    )
    alpha, beta = scal[0, 0], scal[1, 0]
    residual_new = residual - alpha * image
    control_new = control + alpha * direction
    updated_direction = residual_new + beta * direction
    return (control_new, residual_new, updated_direction)


def solution(mesh):
    grid = P(("member", "level"), ("tile", "tm"), None)
    placed = (
        grid,
        grid,
        grid,
        grid,
        P(("member", "level")),
        P(("member", "tile"), "tm", None),
        P(("member", "tile"), "tm", None),
        P(("member", "tile"), "tm"),
        P(("member", "tile"), "tm", None, None),
        P(("member", "tile"), "tm", "level", None),
        P(("member", "tile"), "tm", None),
    )
    sizes = tuple(mesh.shape[axis] for axis in ("tile", "tm", "level"))
    return jax.shard_map(
        functools.partial(local, sizes),
        mesh=mesh,
        in_specs=placed,
        out_specs=(grid, grid, grid),
        check_vma=False,
    )
```

```python
import functools

import jax
import jax.numpy as jnp
from jax import lax
from jax.experimental import pallas as pl
from jax.experimental.pallas import tpu as pltpu
from jax.sharding import PartitionSpec as P

K_DIFF = 4
HALO = K_DIFF
center_coef = 0.1
row_coef = 0.2
level_coef = 0.05
MESH = pl.DeviceIdType.MESH
f32 = jnp.float32
bf16 = jnp.bfloat16


def split(x):
    high = x.astype(bf16)
    return high, (x - high.astype(f32)).astype(bf16)


def kernel(
    sizes,
    residual_h, direction_h, sigma_h, decay, cell_h, slot_h, count, horiz_h, vert_h, prec_h,
    image, scal,
    residual, direction, sigma, cell, slot, horiz, vert, prec, onehots, load_sem,
    a0, a1, t0, t1, top, bot, rd, ru, xd, xu, xc, pack, obs, fields, parts, models,
    acc, ip1,
    halo_send, halo_recv, obs_send, obs_recv, mod_send, mod_recv,
    s1_send, s1_recv,
):
    nt, ntm, nlev = sizes
    levels, rows, width = direction.shape
    blocks = cell.shape[1]
    ng, ngroup = nt * ntm, ntm * nlev
    keep = onehots.shape[0] > 1
    member = lax.axis_index("member")
    tile = lax.axis_index("tile")
    tm = lax.axis_index("tm")
    lev = lax.axis_index("level")
    g = tile * ntm + tm
    other = 1 - lev
    has_up, has_down = g > 0, g < ng - 1

    def dev(index, level):
        return (member, index // ntm, lax.rem(index, ntm), level)

    loads = [
        pltpu.make_async_copy(src, dst, load_sem.at[n])
        for n, (src, dst) in enumerate(
            [
                (direction_h, direction), (vert_h, vert), (horiz_h, horiz), (cell_h, cell),
                (slot_h, slot), (prec_h, prec), (sigma_h, sigma), (residual_h, residual),
            ]
        )
    ]
    for load in loads:
        load.start()

    barrier = pltpu.get_barrier_semaphore()
    everyone = ng * nlev
    me = g * nlev + lev
    for i in range(1, everyone):
        to = lax.rem(me + i, everyone)
        pl.semaphore_signal(
            barrier, inc=1, device_id=dev(to // nlev, lax.rem(to, nlev)), device_id_type=MESH
        )

    sub = lax.broadcasted_iota(jnp.int32, (rows, width), 0)
    low_half = sub < HALO

    def pack_rows(source, base):
        for j in range(levels // 2):
            even, odd = source[base + 2 * j], pltpu.roll(source[base + 2 * j + 1], HALO, 0)
            top[j] = jnp.where(low_half, even, odd)
            bot[j] = jnp.where(low_half, odd, even)

    pairs = levels // 2

    def halo_copies(phase, source, base):
        up, down = g - 1, g + 1
        half = pl.ds(2 * other, 2)
        edge = pl.ds(base + HALO * other, HALO)
        plan = []
        for c in range(pairs):
            j = c + lev * (pairs - 1 - 2 * c)
            plan.append((top.at[j], rd.at[phase, j], up, lev, has_up, has_down))
            plan.append((bot.at[j], ru.at[phase, j], down, lev, has_down, has_up))
        plan += [
            (source.at[edge], xc.at[phase], g, other, None, None),
            (rd.at[phase].at[half], xd.at[phase], g, other, has_down, has_down),
            (ru.at[phase].at[half], xu.at[phase], g, other, has_up, has_up),
        ]
        return [
            (
                pltpu.make_async_remote_copy(
                    src_ref=src, dst_ref=dst,
                    send_sem=halo_send.at[phase, n], recv_sem=halo_recv.at[phase, n],
                    device_id=dev(jnp.clip(to, 0, ng - 1), level), device_id_type=MESH,
                ),
                sends, gets,
            )
            for n, (src, dst, to, level, sends, gets) in enumerate(plan)
        ]

    def when(condition, action):
        if condition is None:
            action()
        else:
            pl.when(condition)(action)

    loads[0].wait()
    pack_rows(direction, 0)
    for load in loads[1:6]:
        load.wait()

    eff_rows = blocks * levels
    h_rows = eff_rows + blocks * 4
    level_id = lax.broadcasted_iota(jnp.int32, (levels, 128), 0)
    lane = lax.broadcasted_iota(jnp.int32, (1, 128), 1)
    rate = jnp.zeros((levels, 128), f32)
    for l in range(levels):
        rate = jnp.where(level_id == l, decay[l], rate)

    def pack_tile(t, carry):
        for b in range(blocks):
            s = slot[t, b : b + 1, :].astype(f32)
            pack[t, b * levels : (b + 1) * levels, :] = vert[t, b] * jnp.exp(-s * rate)
            pack[t, eff_rows + 4 * b : eff_rows + 4 * b + 4, :] = horiz[t, b]
            pack[t, h_rows + b : h_rows + b + 1, :] = jnp.where(
                lane < count[t, b], prec[t, b : b + 1, :], 0.0
            )
        pack[t, h_rows + blocks : h_rows + 2 * blocks, :] = cell[t].astype(f32)
        return carry

    lax.fori_loop(0, nt, pack_tile, 0)
    pl.semaphore_wait(barrier, everyone - 1)
    halo1 = halo_copies(0, direction, 0)
    for copy, sends, gets in halo1[: 2 * pairs + 1]:
        when(sends, copy.start)

    def obs_copy(i):
        to = lax.rem(g + i, ng)
        return pltpu.make_async_remote_copy(
            src_ref=pack.at[to // ntm], dst_ref=obs.at[g],
            send_sem=obs_send.at[i], recv_sem=obs_recv.at[i],
            device_id=dev(to, lev), device_id_type=MESH,
        )

    def obs_arrival(i):
        return pltpu.make_async_remote_copy(
            src_ref=pack.at[tile], dst_ref=obs.at[lax.rem(g - i + ng, ng)],
            send_sem=obs_send.at[i], recv_sem=obs_recv.at[i],
            device_id=dev(lax.rem(g + i, ng), lev), device_id_type=MESH,
        )

    for i in range(1, ng):
        obs_copy(i).start()
    obs[g] = pack[tile]

    inside = (low_half & has_down) | (jnp.logical_not(low_half) & has_up)

    def unpack(down, up, at):
        a1[at] = jnp.where(inside, jnp.where(low_half, down, up), 0.0)
        a1[at + 1] = jnp.where(
            inside, pltpu.roll(jnp.where(low_half, up, down), HALO, 0), 0.0
        )

    zero = jnp.zeros((rows, width), f32)
    for buffer in (a0, a1, t0, t1):
        buffer[0] = zero
        buffer[levels + HALO + 1] = zero
    own = 1 + HALO * lev
    far = 1 + levels * other

    def advance(step, w, src0, src1, dst0, dst1):
        place = w - step
        l = 1 + place + lev * (levels + HALO - 1 - 2 * place)
        full = jnp.concatenate([src0[l], src1[l]], axis=0)
        near = (
            pltpu.roll(full, 1, 0) + pltpu.roll(full, 2 * rows - 1, 0)
            + pltpu.roll(full, 1, 1) + pltpu.roll(full, width - 1, 1)
        )
        main = center_coef * full + row_coef * near
        dst0[l] = main[:rows] + level_coef * (src0[l - 1] + src0[l + 1])
        if step < K_DIFF:
            side = main[rows:] + level_coef * (src1[l - 1] + src1[l + 1])
            dst1[l] = jnp.where(inside, side, 0.0)

    def wave(start, end):
        def body(w, carry):
            for step in range(1, K_DIFF + 1):
                to = (t0, t1) if step % 2 else (a0, a1)
                of = (a0, a1) if step % 2 else (t0, t1)
                pl.when(w >= step)(functools.partial(advance, step, w, *of, *to))
            return carry

        lax.fori_loop(start, end, body, 0)

    def smooth(phase, copies):
        for c in range(pairs):
            j = c + lev * (pairs - 1 - 2 * c)
            for n in range(2):
                when(copies[2 * c + n][2], copies[2 * c + n][0].wait_recv)
            if c == pairs - 1:
                for n in range(2):
                    forward = copies[2 * pairs + 1 + n]
                    when(forward[1], forward[0].start)
            unpack(rd[phase, j], ru[phase, j], own + 2 * j)
            if c == 0:
                copies[2 * pairs][0].wait()
            wave(max(1, 2 * c), 2 * c + 2)
        for copy, sends, gets in copies[2 * pairs + 1 :]:
            when(gets, copy.wait_recv)
        for j in range(HALO // 2):
            unpack(xd[phase, j], xu[phase, j], far + 2 * j)
        for l in range(HALO):
            a0[far + l] = xc[phase, l]
        wave(levels, levels + HALO)
        for copy, sends, gets in copies[: 2 * pairs] + copies[2 * pairs + 1 :]:
            when(sends, copy.wait_send)

    a0[pl.ds(own, levels)] = direction[...]
    smooth(0, halo1)

    loads[6].wait()
    cells_here = levels * rows
    increment = (sigma[...] * a0[pl.ds(own, levels)]).reshape(cells_here, width)
    high, low = split(increment)
    fields[0:cells_here] = high
    fields[2 * cells_here : 3 * cells_here] = low
    high, low = split(pltpu.roll(increment, width - 1, 1))
    fields[cells_here : 2 * cells_here] = high
    fields[3 * cells_here : 4 * cells_here] = low

    for i in range(1, ng):
        obs_arrival(i).wait_recv()

    nobs = blocks * 128
    row_id = lax.broadcasted_iota(jnp.int32, (rows, nobs), 0).astype(f32)
    first_row = (tm * rows).astype(f32)

    def lanes(q, start, stride):
        return jnp.concatenate(
            [obs[q, start + b * stride : start + b * stride + 1, :] for b in range(blocks)], axis=1
        )

    def stencil(q):
        c = lanes(q, h_rows + blocks, 1)
        row = jnp.floor((c + 0.5) * (1.0 / width))
        col = (c - row * width).astype(jnp.int32)
        row = row - first_row
        lower, upper = row_id == row, row_id == row + 1.0
        weights = [
            jnp.where(lower, lanes(q, eff_rows + k, 4), 0.0)
            + jnp.where(upper, lanes(q, eff_rows + 2 + k, 4), 0.0)
            for k in range(2)
        ]
        return weights, col

    def matrix(col):
        col_id = lax.broadcasted_iota(jnp.int32, (width, nobs), 0)
        return jnp.where(col_id == col, 1.0, 0.0).astype(bf16)

    def gather(q, carry):
        weights, col = stencil(q)
        onehot = matrix(col)
        if keep:
            onehots[q] = onehot
        values = jnp.dot(fields[...], onehot, preferred_element_type=f32)
        values = values[: 2 * cells_here] + values[2 * cells_here :]
        total = jnp.zeros((rows, nobs), f32)
        for k in range(2):
            part = jnp.zeros((rows, nobs), f32)
            for l in range(levels):
                at = k * cells_here + l * rows
                part = part + lanes(q, l, levels) * values[at : at + rows]
            total = total + part * weights[k]
        total = jnp.sum(total, axis=0, keepdims=True)
        parts[q] = jnp.concatenate(
            [total[:, 128 * b : 128 * (b + 1)] for b in range(blocks)]
            + [jnp.zeros((8 - blocks, 128), f32)],
            axis=0,
        )
        return carry

    lax.fori_loop(0, ng, gather, 0)

    tg = tm * nlev + lev

    def exchange(i, src, slots, send, recv):
        to = lax.rem(tg + i, ngroup)
        came = lax.rem(tg - i + ngroup, ngroup)
        where = (member, tile, to // nlev, lax.rem(to, nlev))
        return [
            pltpu.make_async_remote_copy(
                src_ref=src, dst_ref=slots.at[at], send_sem=send.at[i], recv_sem=recv.at[i],
                device_id=where, device_id_type=MESH,
            )
            for at in (tg, came)
        ]

    swaps = [exchange(i, parts, models, mod_send, mod_recv) for i in range(1, ngroup)]
    for out, _ in swaps:
        out.start()
    models[tg] = parts[...]
    acc[...] = jnp.zeros_like(acc)
    for _, back in swaps:
        back.wait_recv()

    def scatter(q, carry):
        weights, col = stencil(q)
        onehot = onehots[q] if keep else matrix(col)
        model = models[0, q]
        for k in range(1, ngroup):
            model = model + models[k, q]
        departure = jnp.concatenate([model[b : b + 1] for b in range(blocks)], axis=1)
        departure = departure * lanes(q, h_rows, 1)
        scaled = [lanes(q, l, levels) * departure for l in range(levels)]
        values = jnp.concatenate(
            [scaled[l] * weights[k] for k in range(2) for l in range(levels)], axis=0
        )
        acc[...] += lax.dot_general(
            jnp.concatenate(split(values), axis=0), onehot, (((1,), (1,)), ((), ())),
            preferred_element_type=f32,
        )
        return carry

    lax.fori_loop(0, ng, scatter, 0)
    adjoint = acc[: 2 * cells_here] + acc[2 * cells_here :]
    adjoint = adjoint[:cells_here] + pltpu.roll(adjoint[cells_here:], 1, 1)
    a0[pl.ds(own, levels)] = sigma[...] * adjoint.reshape(levels, rows, width)
    pack_rows(a0, own)
    halo2 = halo_copies(1, a0, own)
    for copy, sends, gets in halo2[: 2 * pairs + 1]:
        when(sends, copy.start)
    smooth(1, halo2)

    loads[7].wait()
    sums = [jnp.zeros((rows, width), f32)] * 4
    for l in range(levels):
        d, r = direction[l], residual[l]
        im = d + a0[own + l]
        image[l] = im
        for n, term in enumerate((r * r, d * im, r * im, im * im)):
            sums[n] = sums[n] + term
    lines = []
    for total in sums:
        total = jnp.sum(total, axis=0, keepdims=True)
        line = total[:, :128]
        for at in range(128, width, 128):
            line = line + total[:, at : at + 128]
        lines.append(line)
    ip1[me] = jnp.concatenate(lines + [jnp.zeros((4, 128), f32)], axis=0)
    swaps1 = []
    for i in range(1, everyone):
        to = lax.rem(me + i, everyone)
        swaps1.append(
            [
                pltpu.make_async_remote_copy(
                    src_ref=ip1.at[me], dst_ref=ip1.at[at],
                    send_sem=s1_send.at[i], recv_sem=s1_recv.at[i],
                    device_id=dev(to // nlev, lax.rem(to, nlev)), device_id_type=MESH,
                )
                for at in (me, lax.rem(me - i + everyone, everyone))
            ]
        )
    for out, _ in swaps1:
        out.start()
    for _, back in swaps1:
        back.wait_recv()
    total = jnp.sum(ip1[...], axis=0)
    total = jnp.broadcast_to(jnp.sum(total, axis=1, keepdims=True), (8, 128))
    norm_old, curvature, cross, image_norm = (total[n : n + 1] for n in range(4))
    alpha = norm_old / curvature
    norm_new = norm_old - 2.0 * alpha * cross + alpha * alpha * image_norm
    scal[...] = jnp.concatenate([alpha, norm_new / norm_old, jnp.zeros((6, 128), f32)], axis=0)

    for i in range(1, ng):
        obs_copy(i).wait_send()
    for out, _ in swaps + swaps1:
        out.wait_send()


def local(
    sizes,
    control,
    residual,
    direction,
    sigma,
    decay_rate,
    obs_cell,
    observation_slot,
    block_count,
    horiz_weight,
    vert_weight,
    obs_precision,
):
    nt, ntm, nlev = sizes
    levels, rows, width = direction.shape
    blocks = obs_cell.shape[1]
    ng, ngroup = nt * ntm, ntm * nlev
    packed = blocks * (levels + 6)
    vmem = pl.BlockSpec(memory_space=pltpu.VMEM)
    hbm = pl.BlockSpec(memory_space=pl.ANY)
    matrices = ng if ng * width * blocks * 128 <= 2**23 else 1
    smem = pl.BlockSpec(memory_space=pltpu.SMEM)
    field = pltpu.VMEM((levels + HALO + 2, rows, width), f32)
    dma = pltpu.SemaphoreType.DMA
    image, scal = pl.pallas_call(
        functools.partial(kernel, sizes),
        out_shape=(
            jax.ShapeDtypeStruct((levels, rows, width), f32),
            jax.ShapeDtypeStruct((8, 128), f32),
        ),
        in_specs=[hbm, hbm, hbm, smem, hbm, hbm, smem, hbm, hbm, hbm],
        out_specs=(vmem, vmem),
        scratch_shapes=[
            *(
                pltpu.VMEM(x.shape, x.dtype)
                for x in (
                    residual, direction, sigma, obs_cell, observation_slot,
                    horiz_weight, vert_weight, obs_precision,
                )
            ),
            pltpu.VMEM((matrices, width, blocks * 128), bf16),
            pltpu.SemaphoreType.DMA((8,)),
            field, field, field, field,
            pltpu.VMEM((levels // 2, rows, width), f32),
            pltpu.VMEM((levels // 2, rows, width), f32),
            pltpu.VMEM((2, levels // 2, rows, width), f32),
            pltpu.VMEM((2, levels // 2, rows, width), f32),
            pltpu.VMEM((2, HALO // 2, rows, width), f32),
            pltpu.VMEM((2, HALO // 2, rows, width), f32),
            pltpu.VMEM((2, HALO, rows, width), f32),
            pltpu.VMEM((nt, packed, 128), f32),
            pltpu.VMEM((ng, packed, 128), f32),
            pltpu.VMEM((4 * levels * rows, width), bf16),
            pltpu.VMEM((ng, 8, 128), f32),
            pltpu.VMEM((ngroup, ng, 8, 128), f32),
            pltpu.VMEM((4 * levels * rows, width), f32),
            pltpu.VMEM((ng * nlev, 8, 128), f32),
            dma((2, levels + 3)), dma((2, levels + 3)),
            dma((ng,)), dma((ng,)),
            dma((ngroup,)), dma((ngroup,)),
            dma((ng * nlev,)), dma((ng * nlev,)),
        ],
        compiler_params=pltpu.CompilerParams(
            collective_id=0, has_side_effects=True, vmem_limit_bytes=60 * 1024 * 1024
        ),
    )(
        residual, direction, sigma, decay_rate, obs_cell, observation_slot, block_count,
        horiz_weight, vert_weight, obs_precision,
    )
    alpha, beta = scal[0, 0], scal[1, 0]
    residual_new = residual - alpha * image
    control_new = control + alpha * direction
    updated_direction = residual_new + beta * direction
    return (control_new, residual_new, updated_direction)


def solution(mesh):
    grid = P(("member", "level"), ("tile", "tm"), None)
    placed = (
        grid,
        grid,
        grid,
        grid,
        P(("member", "level")),
        P(("member", "tile"), "tm", None),
        P(("member", "tile"), "tm", None),
        P(("member", "tile"), "tm"),
        P(("member", "tile"), "tm", None, None),
        P(("member", "tile"), "tm", "level", None),
        P(("member", "tile"), "tm", None),
    )
    sizes = tuple(mesh.shape[axis] for axis in ("tile", "tm", "level"))
    return jax.shard_map(
        functools.partial(local, sizes),
        mesh=mesh,
        in_specs=placed,
        out_specs=(grid, grid, grid),
        check_vma=False,
    )
```

```python
import functools

import jax
import jax.numpy as jnp
from jax import lax
from jax.experimental import pallas as pl
from jax.experimental.pallas import tpu as pltpu
from jax.sharding import PartitionSpec as P

K_DIFF = 4
HALO = K_DIFF
center_coef = 0.1
row_coef = 0.2
level_coef = 0.05
MESH = pl.DeviceIdType.MESH
f32 = jnp.float32
bf16 = jnp.bfloat16


def split(x):
    high = x.astype(bf16)
    return high, (x - high.astype(f32)).astype(bf16)


def kernel(
    sizes,
    residual_h, direction_h, sigma_h, decay, cell_h, slot_h, count, horiz_h, vert_h, prec_h,
    image, scal,
    residual, direction, sigma, cell, slot, horiz, vert, prec, onehots, load_sem,
    a0, a1, t0, t1, top, bot, rd, ru, xd, xu, xc, pack, obs, fields, parts, models,
    acc, ip1,
    halo_send, halo_recv, obs_send, obs_recv, mod_send, mod_recv,
    s1_send, s1_recv,
):
    nt, ntm, nlev = sizes
    levels, rows, width = direction.shape
    blocks = cell.shape[1]
    ng, ngroup = nt * ntm, ntm * nlev
    keep = onehots.shape[0] > 1
    member = lax.axis_index("member")
    tile = lax.axis_index("tile")
    tm = lax.axis_index("tm")
    lev = lax.axis_index("level")
    g = tile * ntm + tm
    other = 1 - lev
    has_up, has_down = g > 0, g < ng - 1

    def dev(index, level):
        return (member, index // ntm, lax.rem(index, ntm), level)

    loads = [
        pltpu.make_async_copy(src, dst, load_sem.at[n])
        for n, (src, dst) in enumerate(
            [
                (direction_h, direction), (vert_h, vert), (horiz_h, horiz), (cell_h, cell),
                (slot_h, slot), (prec_h, prec), (sigma_h, sigma), (residual_h, residual),
            ]
        )
    ]
    for load in loads:
        load.start()

    barrier = pltpu.get_barrier_semaphore()
    everyone = ng * nlev
    me = g * nlev + lev
    for i in range(1, everyone):
        to = lax.rem(me + i, everyone)
        pl.semaphore_signal(
            barrier, inc=1, device_id=dev(to // nlev, lax.rem(to, nlev)), device_id_type=MESH
        )

    sub = lax.broadcasted_iota(jnp.int32, (rows, width), 0)
    low_half = sub < HALO

    def pack_rows(source, base):
        for j in range(levels // 2):
            even, odd = source[base + 2 * j], pltpu.roll(source[base + 2 * j + 1], HALO, 0)
            top[j] = jnp.where(low_half, even, odd)
            bot[j] = jnp.where(low_half, odd, even)

    pairs = levels // 2

    def halo_copies(phase, source, base):
        up, down = g - 1, g + 1
        half = pl.ds(2 * other, 2)
        edge = pl.ds(base + HALO * other, HALO)
        plan = []
        for c in range(pairs):
            j = c + lev * (pairs - 1 - 2 * c)
            plan.append((top.at[j], rd.at[phase, j], up, lev, has_up, has_down))
            plan.append((bot.at[j], ru.at[phase, j], down, lev, has_down, has_up))
        plan += [
            (source.at[edge], xc.at[phase], g, other, None, None),
            (rd.at[phase].at[half], xd.at[phase], g, other, has_down, has_down),
            (ru.at[phase].at[half], xu.at[phase], g, other, has_up, has_up),
        ]
        return [
            (
                pltpu.make_async_remote_copy(
                    src_ref=src, dst_ref=dst,
                    send_sem=halo_send.at[phase, n], recv_sem=halo_recv.at[phase, n],
                    device_id=dev(jnp.clip(to, 0, ng - 1), level), device_id_type=MESH,
                ),
                sends, gets,
            )
            for n, (src, dst, to, level, sends, gets) in enumerate(plan)
        ]

    def when(condition, action):
        if condition is None:
            action()
        else:
            pl.when(condition)(action)

    loads[0].wait()
    pack_rows(direction, 0)
    for load in loads[1:6]:
        load.wait()

    eff_rows = blocks * levels
    h_rows = eff_rows + blocks * 4
    level_id = lax.broadcasted_iota(jnp.int32, (levels, 128), 0)
    lane = lax.broadcasted_iota(jnp.int32, (1, 128), 1)
    rate = jnp.zeros((levels, 128), f32)
    for l in range(levels):
        rate = jnp.where(level_id == l, decay[l], rate)

    def pack_tile(t, carry):
        for b in range(blocks):
            s = slot[t, b : b + 1, :].astype(f32)
            pack[t, b * levels : (b + 1) * levels, :] = vert[t, b] * jnp.exp(-s * rate)
            pack[t, eff_rows + 4 * b : eff_rows + 4 * b + 4, :] = horiz[t, b]
            pack[t, h_rows + b : h_rows + b + 1, :] = jnp.where(
                lane < count[t, b], prec[t, b : b + 1, :], 0.0
            )
        pack[t, h_rows + blocks : h_rows + 2 * blocks, :] = cell[t].astype(f32)
        return carry

    lax.fori_loop(0, nt, pack_tile, 0)
    pl.semaphore_wait(barrier, everyone - 1)
    halo1 = halo_copies(0, direction, 0)
    for copy, sends, gets in halo1[: 2 * pairs + 1]:
        when(sends, copy.start)

    def obs_copy(i):
        to = lax.rem(g + i, ng)
        return pltpu.make_async_remote_copy(
            src_ref=pack.at[to // ntm], dst_ref=obs.at[g],
            send_sem=obs_send.at[i], recv_sem=obs_recv.at[i],
            device_id=dev(to, lev), device_id_type=MESH,
        )

    def obs_arrival(i):
        return pltpu.make_async_remote_copy(
            src_ref=pack.at[tile], dst_ref=obs.at[lax.rem(g - i + ng, ng)],
            send_sem=obs_send.at[i], recv_sem=obs_recv.at[i],
            device_id=dev(lax.rem(g + i, ng), lev), device_id_type=MESH,
        )

    for i in range(1, ng):
        obs_copy(i).start()
    obs[g] = pack[tile]

    inside = (low_half & has_down) | (jnp.logical_not(low_half) & has_up)

    def unpack(down, up, at):
        a1[at] = jnp.where(inside, jnp.where(low_half, down, up), 0.0)
        a1[at + 1] = jnp.where(
            inside, pltpu.roll(jnp.where(low_half, up, down), HALO, 0), 0.0
        )

    zero = jnp.zeros((rows, width), f32)
    for buffer in (a0, a1, t0, t1):
        buffer[0] = zero
        buffer[levels + HALO + 1] = zero
    own = 1 + HALO * lev
    far = 1 + levels * other

    def advance(step, w, src0, src1, dst0, dst1):
        place = w - step
        l = 1 + place + lev * (levels + HALO - 1 - 2 * place)
        full = jnp.concatenate([src0[l], src1[l]], axis=0)
        near = (
            pltpu.roll(full, 1, 0) + pltpu.roll(full, 2 * rows - 1, 0)
            + pltpu.roll(full, 1, 1) + pltpu.roll(full, width - 1, 1)
        )
        main = center_coef * full + row_coef * near
        dst0[l] = main[:rows] + level_coef * (src0[l - 1] + src0[l + 1])
        if step < K_DIFF:
            side = main[rows:] + level_coef * (src1[l - 1] + src1[l + 1])
            dst1[l] = jnp.where(inside, side, 0.0)

    def wave(start, end):
        def body(w, carry):
            for step in range(1, K_DIFF + 1):
                to = (t0, t1) if step % 2 else (a0, a1)
                of = (a0, a1) if step % 2 else (t0, t1)
                pl.when(w >= step)(functools.partial(advance, step, w, *of, *to))
            return carry

        lax.fori_loop(start, end, body, 0)

    def smooth(phase, copies):
        for c in range(pairs):
            j = c + lev * (pairs - 1 - 2 * c)
            for n in range(2):
                when(copies[2 * c + n][2], copies[2 * c + n][0].wait_recv)
            if c == pairs - 1:
                for n in range(2):
                    forward = copies[2 * pairs + 1 + n]
                    when(forward[1], forward[0].start)
            unpack(rd[phase, j], ru[phase, j], own + 2 * j)
            if c == 0:
                copies[2 * pairs][0].wait()
            wave(max(1, 2 * c), 2 * c + 2)
        for copy, sends, gets in copies[2 * pairs + 1 :]:
            when(gets, copy.wait_recv)
        for j in range(HALO // 2):
            unpack(xd[phase, j], xu[phase, j], far + 2 * j)
        for l in range(HALO):
            a0[far + l] = xc[phase, l]
        wave(levels, levels + HALO)
        for copy, sends, gets in copies[: 2 * pairs] + copies[2 * pairs + 1 :]:
            when(sends, copy.wait_send)

    a0[pl.ds(own, levels)] = direction[...]
    smooth(0, halo1)

    loads[6].wait()
    cells_here = levels * rows
    increment = (sigma[...] * a0[pl.ds(own, levels)]).reshape(cells_here, width)
    high, low = split(increment)
    fields[0:cells_here] = high
    fields[2 * cells_here : 3 * cells_here] = low
    high, low = split(pltpu.roll(increment, width - 1, 1))
    fields[cells_here : 2 * cells_here] = high
    fields[3 * cells_here : 4 * cells_here] = low

    for i in range(1, ng):
        obs_arrival(i).wait_recv()

    nobs = blocks * 128
    row_id = lax.broadcasted_iota(jnp.int32, (rows, nobs), 0).astype(f32)
    first_row = (tm * rows).astype(f32)

    def lanes(q, start, stride):
        return jnp.concatenate(
            [obs[q, start + b * stride : start + b * stride + 1, :] for b in range(blocks)], axis=1
        )

    def stencil(q):
        c = lanes(q, h_rows + blocks, 1)
        row = jnp.floor((c + 0.5) * (1.0 / width))
        col = (c - row * width).astype(jnp.int32)
        row = row - first_row
        lower, upper = row_id == row, row_id == row + 1.0
        weights = [
            jnp.where(lower, lanes(q, eff_rows + k, 4), 0.0)
            + jnp.where(upper, lanes(q, eff_rows + 2 + k, 4), 0.0)
            for k in range(2)
        ]
        return weights, col

    def matrix(col):
        col_id = lax.broadcasted_iota(jnp.int32, (width, nobs), 0)
        return jnp.where(col_id == col, 1.0, 0.0).astype(bf16)

    def gather(q, carry):
        weights, col = stencil(q)
        onehot = matrix(col)
        if keep:
            onehots[q] = onehot
        values = jnp.dot(fields[...], onehot, preferred_element_type=f32)
        values = values[: 2 * cells_here] + values[2 * cells_here :]
        total = jnp.zeros((rows, nobs), f32)
        for k in range(2):
            part = jnp.zeros((rows, nobs), f32)
            for l in range(levels):
                at = k * cells_here + l * rows
                part = part + lanes(q, l, levels) * values[at : at + rows]
            total = total + part * weights[k]
        total = jnp.sum(total, axis=0, keepdims=True)
        parts[q] = jnp.concatenate(
            [total[:, 128 * b : 128 * (b + 1)] for b in range(blocks)]
            + [jnp.zeros((8 - blocks, 128), f32)],
            axis=0,
        )
        return carry

    lax.fori_loop(0, ng, gather, 0)

    tg = tm * nlev + lev

    def exchange(i, src, slots, send, recv):
        to = lax.rem(tg + i, ngroup)
        came = lax.rem(tg - i + ngroup, ngroup)
        where = (member, tile, to // nlev, lax.rem(to, nlev))
        return [
            pltpu.make_async_remote_copy(
                src_ref=src, dst_ref=slots.at[at], send_sem=send.at[i], recv_sem=recv.at[i],
                device_id=where, device_id_type=MESH,
            )
            for at in (tg, came)
        ]

    swaps = [exchange(i, parts, models, mod_send, mod_recv) for i in range(1, ngroup)]
    for out, _ in swaps:
        out.start()
    models[tg] = parts[...]
    acc[...] = jnp.zeros_like(acc)
    for _, back in swaps:
        back.wait_recv()

    def scatter(q, carry):
        weights, col = stencil(q)
        onehot = onehots[q] if keep else matrix(col)
        model = models[0, q]
        for k in range(1, ngroup):
            model = model + models[k, q]
        departure = jnp.concatenate([model[b : b + 1] for b in range(blocks)], axis=1)
        departure = departure * lanes(q, h_rows, 1)
        scaled = [lanes(q, l, levels) * departure for l in range(levels)]
        values = jnp.concatenate(
            [scaled[l] * weights[k] for k in range(2) for l in range(levels)], axis=0
        )
        acc[...] += lax.dot_general(
            jnp.concatenate(split(values), axis=0), onehot, (((1,), (1,)), ((), ())),
            preferred_element_type=f32,
        )
        return carry

    lax.fori_loop(0, ng, scatter, 0)
    halo2 = halo_copies(1, a0, own)
    for c in range(pairs):
        j = c + lev * (pairs - 1 - 2 * c)
        for n in range(2):
            l = 2 * j + n
            quarters = [
                acc[pl.ds(pl.multiple_of(k * cells_here + l * rows, rows), rows)] for k in range(4)
            ]
            shifted = pltpu.roll(quarters[1] + quarters[3], 1, 1)
            a0[own + l] = sigma[l] * (quarters[0] + quarters[2] + shifted)
        even, odd = a0[own + 2 * j], pltpu.roll(a0[own + 2 * j + 1], HALO, 0)
        top[j] = jnp.where(low_half, even, odd)
        bot[j] = jnp.where(low_half, odd, even)
        for copy, sends, gets in halo2[2 * c : 2 * c + 2]:
            when(sends, copy.start)
    halo2[2 * pairs][0].start()
    smooth(1, halo2)

    loads[7].wait()
    sums = [jnp.zeros((rows, width), f32)] * 4
    for l in range(levels):
        d, r = direction[l], residual[l]
        im = d + a0[own + l]
        image[l] = im
        for n, term in enumerate((r * r, d * im, r * im, im * im)):
            sums[n] = sums[n] + term
    lines = []
    for total in sums:
        total = jnp.sum(total, axis=0, keepdims=True)
        line = total[:, :128]
        for at in range(128, width, 128):
            line = line + total[:, at : at + 128]
        lines.append(line)
    ip1[me] = jnp.concatenate(lines + [jnp.zeros((4, 128), f32)], axis=0)
    swaps1 = []
    for i in range(1, everyone):
        to = lax.rem(me + i, everyone)
        swaps1.append(
            [
                pltpu.make_async_remote_copy(
                    src_ref=ip1.at[me], dst_ref=ip1.at[at],
                    send_sem=s1_send.at[i], recv_sem=s1_recv.at[i],
                    device_id=dev(to // nlev, lax.rem(to, nlev)), device_id_type=MESH,
                )
                for at in (me, lax.rem(me - i + everyone, everyone))
            ]
        )
    for out, _ in swaps1:
        out.start()
    for _, back in swaps1:
        back.wait_recv()
    total = jnp.sum(ip1[...], axis=0)
    total = jnp.broadcast_to(jnp.sum(total, axis=1, keepdims=True), (8, 128))
    norm_old, curvature, cross, image_norm = (total[n : n + 1] for n in range(4))
    alpha = norm_old / curvature
    norm_new = norm_old - 2.0 * alpha * cross + alpha * alpha * image_norm
    scal[...] = jnp.concatenate([alpha, norm_new / norm_old, jnp.zeros((6, 128), f32)], axis=0)

    for i in range(1, ng):
        obs_copy(i).wait_send()
    for out, _ in swaps + swaps1:
        out.wait_send()


def local(
    sizes,
    control,
    residual,
    direction,
    sigma,
    decay_rate,
    obs_cell,
    observation_slot,
    block_count,
    horiz_weight,
    vert_weight,
    obs_precision,
):
    nt, ntm, nlev = sizes
    levels, rows, width = direction.shape
    blocks = obs_cell.shape[1]
    ng, ngroup = nt * ntm, ntm * nlev
    packed = blocks * (levels + 6)
    vmem = pl.BlockSpec(memory_space=pltpu.VMEM)
    hbm = pl.BlockSpec(memory_space=pl.ANY)
    matrices = ng if ng * width * blocks * 128 <= 2**23 else 1
    smem = pl.BlockSpec(memory_space=pltpu.SMEM)
    field = pltpu.VMEM((levels + HALO + 2, rows, width), f32)
    dma = pltpu.SemaphoreType.DMA
    image, scal = pl.pallas_call(
        functools.partial(kernel, sizes),
        out_shape=(
            jax.ShapeDtypeStruct((levels, rows, width), f32),
            jax.ShapeDtypeStruct((8, 128), f32),
        ),
        in_specs=[hbm, hbm, hbm, smem, hbm, hbm, smem, hbm, hbm, hbm],
        out_specs=(vmem, vmem),
        scratch_shapes=[
            *(
                pltpu.VMEM(x.shape, x.dtype)
                for x in (
                    residual, direction, sigma, obs_cell, observation_slot,
                    horiz_weight, vert_weight, obs_precision,
                )
            ),
            pltpu.VMEM((matrices, width, blocks * 128), bf16),
            pltpu.SemaphoreType.DMA((8,)),
            field, field, field, field,
            pltpu.VMEM((levels // 2, rows, width), f32),
            pltpu.VMEM((levels // 2, rows, width), f32),
            pltpu.VMEM((2, levels // 2, rows, width), f32),
            pltpu.VMEM((2, levels // 2, rows, width), f32),
            pltpu.VMEM((2, HALO // 2, rows, width), f32),
            pltpu.VMEM((2, HALO // 2, rows, width), f32),
            pltpu.VMEM((2, HALO, rows, width), f32),
            pltpu.VMEM((nt, packed, 128), f32),
            pltpu.VMEM((ng, packed, 128), f32),
            pltpu.VMEM((4 * levels * rows, width), bf16),
            pltpu.VMEM((ng, 8, 128), f32),
            pltpu.VMEM((ngroup, ng, 8, 128), f32),
            pltpu.VMEM((4 * levels * rows, width), f32),
            pltpu.VMEM((ng * nlev, 8, 128), f32),
            dma((2, levels + 3)), dma((2, levels + 3)),
            dma((ng,)), dma((ng,)),
            dma((ngroup,)), dma((ngroup,)),
            dma((ng * nlev,)), dma((ng * nlev,)),
        ],
        compiler_params=pltpu.CompilerParams(
            collective_id=0, has_side_effects=True, vmem_limit_bytes=60 * 1024 * 1024
        ),
    )(
        residual, direction, sigma, decay_rate, obs_cell, observation_slot, block_count,
        horiz_weight, vert_weight, obs_precision,
    )
    alpha, beta = scal[0, 0], scal[1, 0]
    residual_new = residual - alpha * image
    control_new = control + alpha * direction
    updated_direction = residual_new + beta * direction
    return (control_new, residual_new, updated_direction)


def solution(mesh):
    grid = P(("member", "level"), ("tile", "tm"), None)
    placed = (
        grid,
        grid,
        grid,
        grid,
        P(("member", "level")),
        P(("member", "tile"), "tm", None),
        P(("member", "tile"), "tm", None),
        P(("member", "tile"), "tm"),
        P(("member", "tile"), "tm", None, None),
        P(("member", "tile"), "tm", "level", None),
        P(("member", "tile"), "tm", None),
    )
    sizes = tuple(mesh.shape[axis] for axis in ("tile", "tm", "level"))
    return jax.shard_map(
        functools.partial(local, sizes),
        mesh=mesh,
        in_specs=placed,
        out_specs=(grid, grid, grid),
        check_vma=False,
    )
```
